32 devices in a mesh: parts: 2 (over y), block: 4 (over z), shot: 2 (over x), sub: 2 (over core).
Axes of the slice: x: 2, y: 2, z: 4, core: 2. Of those that a mesh axis runs over, the one named last changes fastest.
Arguments:
- vel_sq: float32 [8, 16, 16, 128], P(('parts', 'block'), None, 'sub'), parts along dimension 0, may hold values from 0.06 to 0.18
- fwd_state: bfloat16 [16, 2, 80, 16, 128], P(('parts', 'block', 'shot'), None, None, 'sub'), parts along dimension 0, may hold values from -6 to 6
- adj_state: bfloat16 [16, 2, 80, 16, 128], P(('parts', 'block', 'shot'), None, None, 'sub'), parts along dimension 0, may hold values from -6 to 6
- wavelet: float32 [16, 4], P(('parts', 'block', 'shot')), parts along dimension 0, may hold values from -12 to 12
- source: int32 [16, 3], P(('parts', 'block', 'shot')), parts along dimension 0, may hold values from 0 to 127, as said below
- aperture: int32 [16, 2], P(('parts', 'block', 'shot')), parts along dimension 0, may hold values from 0 to 2
- rec_mask: int32 [16, 80, 16], P(('parts', 'block', 'shot'), None, 'sub'), parts along dimension 0, may hold values 0 or 1
- rec_data: float32 [16, 4, 80, 16], P(('parts', 'block', 'shot'), None, None, 'sub'), parts along dimension 0, may hold values from -6 to 6
Outputs:
- image: float32 [8, 16, 16, 128], P(('parts', 'block'), None, 'sub', 'shot'), parts along dimension 0
The draws below stay inside these ranges and needn't reach their ends.
There are 2 independent parts, one for each index of `parts`. The reference program is written for one: setup_inputs(seed, part) draws one part's arguments, and reference() takes and returns one part's arrays. A program takes and returns all parts, laid end to end along the dimension named above; each array names one. Nothing has to cross between parts.
Inputs may be any that keep to these rules, and one draw needn't show every extreme that they name: source offsets lie in the home block, second coordinate below 16, depth below 128.
All inputs are finite; a program needn't handle non-finite values. No bound on the sum of `rec_mask` on one device may be relied on, other than what follows from the above.
Results may differ from the reference program's by a relative error of at most 0.0003.
Values may be sent and summed in bfloat16 or wider, within the bound.
A program may use at most 64 MiB of HBM per device.

```python
import math
import jax
import jax.numpy as jnp
from jax import lax

BX = 16
BY = 16
BZ = 128
R = 2
STEPS = 4
NBLK = 4
SHOTS = 8
WX = 80
N_SHOT = 2


def draw_source(key, part):
    key = jax.random.fold_in(key, 7)
    keys = jax.random.split(key, 3)
    along = jax.random.randint(keys[0], (SHOTS,), 0, BX)
    across = jax.random.randint(keys[1], (SHOTS,), 0, BY)
    depth = jax.random.randint(keys[2], (SHOTS,), 0, BZ)
    return jnp.stack([along, across, depth], 1).astype(jnp.int32)


def set_ends(entries, own_key, least, top_value):
    place = [jax.random.randint(jax.random.fold_in(own_key, axis), (), 0, length) for axis, length in enumerate(entries.shape)]
    longest = entries.shape.index(max(entries.shape))
    neighbour = place[:longest] + [(place[longest] + 1) % entries.shape[longest]] + place[longest + 1:]
    return entries.at[tuple(place)].set(least).at[tuple(neighbour)].set(top_value)


def level_of(rng, shape, pieces, low, top_value):
    loudness, own = 1.0, jax.random.fold_in(rng, 6)
    for position, blocks in pieces:
        draws = jnp.exp(jax.random.uniform(jax.random.fold_in(own, position), (blocks,), jnp.float32, low / len(pieces), top_value / len(pieces)))
        loudness = loudness * jnp.repeat(draws, shape[position] // blocks).reshape([-1 if axis == position else 1 for axis in range(len(shape))])
    return loudness


def centred(stream_key, shape, spread, most, cuts=(), kind=jnp.bfloat16):
    result = jax.random.normal(stream_key, shape, jnp.float32) * spread
    if len(cuts) > 0:
        result = level_of(stream_key, shape, cuts, -0.22, 0.18) * result
    return jnp.clip(result, min=-most, max=most).astype(kind)


def setup_inputs(seed: int = 0, part: int = 0) -> dict:
    seeds = jax.random.split(jax.random.key(seed), 9)
    part_keys = jax.random.split(jax.random.fold_in(seeds[8], part), 9)
    return {
        "vel_sq": jnp.clip(jnp.exp(math.log(0.18) - 1.09861235 * jax.random.uniform(part_keys[0], (NBLK, BX, BY, BZ), jnp.float32) ** level_of(part_keys[0], (NBLK, BX, BY, BZ), ((0, 4), (2, 2)), -0.2, 0.2)), 0.06, 0.18),
        "fwd_state": centred(part_keys[1], (SHOTS, 2, WX, BY, BZ), 1.0, 6.0, ((0, 8), (3, 2))),
        "adj_state": centred(part_keys[2], (SHOTS, 2, WX, BY, BZ), 1.0, 6.0, ((0, 8), (3, 2))),
        "wavelet": centred(part_keys[3], (SHOTS, STEPS), 3.0, 12.0, ((0, 8),), jnp.float32),
        "source": draw_source(jax.random.fold_in(jax.random.fold_in(seeds[8], part), 71), part),
        "aperture": set_ends(jax.random.randint(part_keys[5], (SHOTS, 2), 0, R + 1), jax.random.fold_in(part_keys[5], 1), 0, R).astype(jnp.int32),
        "rec_mask": set_ends((jax.random.randint(part_keys[6], (SHOTS, WX, BY), 0, 4) < 3).astype(jnp.int32), jax.random.fold_in(part_keys[6], 1), 0, 1),
        "rec_data": centred(part_keys[7], (SHOTS, STEPS, WX, BY), 1.0, 6.0, ((0, 8), (3, 2)), jnp.float32),
    }


coeffs = (-205.0 / 72.0, 8.0 / 5.0, -1.0 / 5.0, 8.0 / 315.0, -1.0 / 560.0)
image_scale = 0.05


def laplace(field):
    sx, sy, sz = field.shape
    padded = jnp.pad(field, 4)
    total = 3.0 * coeffs[0] * field
    for step in range(1, 5):
        total = total + coeffs[step] * (padded[4 + step:4 + step + sx, 4:4 + sy, 4:4 + sz] + padded[4 - step:4 - step + sx, 4:4 + sy, 4:4 + sz])
        total = total + coeffs[step] * (padded[4:4 + sx, 4 + step:4 + step + sy, 4:4 + sz] + padded[4:4 + sx, 4 - step:4 - step + sy, 4:4 + sz])
        total = total + coeffs[step] * (padded[4:4 + sx, 4:4 + sy, 4 + step:4 + step + sz] + padded[4:4 + sx, 4:4 + sy, 4 - step:4 - step + sz])
    return total


def one_shot(window, home, fwd, adj, wav, src, ap, rmask, rdata):
    blocks = 2 * R + 1
    index = jnp.arange(blocks, dtype=jnp.int32)
    inside = (index >= R - ap[0]) & (index <= R + ap[1]) & (home - R + index >= 0) & (home - R + index < NBLK)
    keep = jnp.repeat(inside.astype(jnp.float32), BX)[:, None, None]
    xpos = lax.broadcasted_iota(jnp.int32, (WX, BY, BZ), 0)
    ypos = lax.broadcasted_iota(jnp.int32, (WX, BY, BZ), 1)
    zpos = lax.broadcasted_iota(jnp.int32, (WX, BY, BZ), 2)
    onehot = ((xpos == R * BX + src[0]) & (ypos == src[1]) & (zpos == src[2])).astype(jnp.float32)
    surface = (jnp.arange(BZ) == 0).astype(jnp.float32)[None, None, :]
    f_prev = keep * fwd[0].astype(jnp.float32)
    f_now = keep * fwd[1].astype(jnp.float32)
    stored = [f_now]
    for step in range(STEPS):
        f_next = keep * (2.0 * f_now - f_prev + window * laplace(f_now) + wav[step] * onehot)
        f_prev, f_now = f_now, f_next
        stored.append(f_now)
    a_next = keep * adj[0].astype(jnp.float32)
    a_now = keep * adj[1].astype(jnp.float32)
    partial_value = stored[STEPS] * a_now
    for step in range(STEPS):
        later = STEPS - 1 - step
        inject = (rmask.astype(jnp.float32) * rdata[later])[:, :, None] * surface
        a_prev = keep * (2.0 * a_now - a_next + window * laplace(a_now) + inject)
        a_next, a_now = a_now, a_prev
        partial_value = partial_value + stored[later] * a_now
    return partial_value


def reference(vel_sq, fwd_state, adj_state, wavelet, source, aperture, rec_mask, rec_data):
    blocks = 2 * R + 1
    zero_blocks = jnp.zeros((R, BX, BY, BZ), jnp.float32)
    vel_pad = jnp.concatenate([zero_blocks, vel_sq, zero_blocks], 0)

    def visit(image_pad, items):
        shot_id, fwd, adj, wav, src, ap, rmask, rdata = items
        home = (shot_id // N_SHOT).astype(jnp.int32)
        window = lax.dynamic_slice_in_dim(vel_pad, home, blocks, 0).reshape(WX, BY, BZ)
        partial_value = one_shot(window, home, fwd, adj, wav, src, ap, rmask, rdata).reshape(blocks, BX, BY, BZ)
        current = lax.dynamic_slice_in_dim(image_pad, home, blocks, 0)
        return lax.dynamic_update_slice_in_dim(image_pad, current + partial_value, home, 0), None

    image_pad = jnp.zeros((NBLK + 2 * R, BX, BY, BZ), jnp.float32)
    shot_ids = jnp.arange(SHOTS, dtype=jnp.int32)
    image_pad, unused = lax.scan(visit, image_pad, (shot_ids, fwd_state, adj_state, wavelet, source, aperture, rec_mask, rec_data))
    return image_scale * image_pad[R:R + NBLK]
```

```python
import functools

import jax
import jax.numpy as jnp
from jax import lax
from jax.experimental import pallas as pl
from jax.experimental.pallas import tpu as pltpu
from jax.sharding import PartitionSpec as P

R = 2
STEPS = 4
NB = 2 * R + 1
MESH = pl.DeviceIdType.MESH

coeffs = (-205.0 / 72.0, 8.0 / 5.0, -1.0 / 5.0, 8.0 / 315.0, -1.0 / 560.0)
image_scale = 0.05
f32 = jnp.float32
bf16 = jnp.bfloat16


def kernel(nblock, nshot, vel, fwd, adj, wav, src, ap, mask, rec, out,
           F, A, W, ZF, ZA, PV, O, T, B, G, S, H,
           vs, vr, fs, fr, as_, ar, gs, gr, ss, sr):
    bx, bys, bz = vel.shape
    home = lax.axis_index("block")
    team = lax.axis_index("shot")
    sub = lax.axis_index("sub")
    lo = jnp.maximum(R - home, 0)
    hi = jnp.minimum(R + nblock - home, NB)
    offsets = [o for o in range(-R, R + 1) if o != 0]

    def near(o):
        return (home + o >= 0) & (home + o < nblock)

    barrier = pltpu.get_barrier_semaphore()
    for o in offsets:
        @pl.when(near(o))
        def _():
            pl.semaphore_signal(barrier, inc=1, device_id={"block": home + o}, device_id_type=MESH)
    for r in range(1, nshot):
        pl.semaphore_signal(barrier, inc=1, device_id={"shot": lax.rem(team + r, nshot)}, device_id_type=MESH)
    pl.semaphore_signal(barrier, inc=1, device_id={"sub": 1 - sub}, device_id_type=MESH)

    def keep_of(b):
        return jnp.where((b >= R - ap[0, 0]) & (b <= R + ap[0, 1]), 1.0, 0.0).astype(f32)

    def at(field, t, b):
        return field[t, pl.ds(4 + b * bx, bx), 8:16, :]

    zx = jnp.zeros((4, 8, bz), f32)

    @pl.when(sub == 0)
    def _():
        lax.fori_loop(lo, hi, functools.partial(clear_at, F, A, 0, bx, bz), 0)

    @pl.when(sub == 1)
    def _():
        lax.fori_loop(lo, hi, functools.partial(clear_at, F, A, 16, bx, bz), 0)

    for field in (F, A):
        for t in range(STEPS):
            field[t, pl.ds(lo * bx, 4), 8:16, :] = zx
            field[t, pl.ds(4 + hi * bx, 4), 8:16, :] = zx

    def load_states(b, c):
        kb = keep_of(b)
        rows = pl.ds(4 + b * bx, bx)
        F[0, rows, 8:16, :] = kb * fwd[1, pl.ds(b * bx, bx)].astype(f32)
        A[0, rows, 8:16, :] = kb * adj[1, pl.ds(b * bx, bx)].astype(f32)
        return c

    lax.fori_loop(lo, hi, load_states, 0)

    count = (hi - lo - 1) + (nshot - 1) + 1
    pl.semaphore_wait(barrier, count)

    def vel_copy(o):
        j = R - o
        return pltpu.make_async_remote_copy(
            src_ref=vel, dst_ref=W.at[pl.ds(j * bx, bx)], send_sem=vs.at[j], recv_sem=vr.at[j],
            device_id={"block": home + o}, device_id_type=MESH)

    def rim_copy(field, t, ssem, rsem):
        x = NB * bx
        return pltpu.make_async_remote_copy(
            src_ref=field.at[t, pl.ds(4, x), pl.ds(8, 8), :],
            dst_ref=field.at[t, pl.ds(4, x), pl.ds(pl.multiple_of(16 * sub, 8), 8), :],
            send_sem=ssem.at[t], recv_sem=rsem.at[t],
            device_id={"sub": 1 - sub}, device_id_type=MESH)

    rim_copy(F, 0, fs, fr).start()
    rim_copy(A, 0, as_, ar).start()
    for o in (-2, 2, -1, 1):
        @pl.when(near(o))
        def _():
            vel_copy(o).start()

    i0 = lax.broadcasted_iota(jnp.int32, (bz, bz), 0)
    i1 = lax.broadcasted_iota(jnp.int32, (bz, bz), 1)
    dist = jnp.abs(i0 - i1)
    band = jnp.where(dist == 0, 3.0 * coeffs[0], 0.0).astype(f32)
    for j in range(1, 5):
        band = jnp.where(dist == j, coeffs[j], band)
    band_hi = band.astype(bf16)
    band_lo = (band - band_hi.astype(f32)).astype(bf16)
    B[0:bz, 0:bz] = band_hi
    B[bz:2 * bz, 0:bz] = band_hi
    B[0:bz, bz:2 * bz] = band_lo
    B[bz:2 * bz, bz:2 * bz] = jnp.zeros((bz, bz), bf16)

    ox = lax.broadcasted_iota(jnp.int32, (bx, bys, bz), 0)
    oy = lax.broadcasted_iota(jnp.int32, (bx, bys, bz), 1) + sub * bys
    oz = lax.broadcasted_iota(jnp.int32, (bx, bys, bz), 2)
    O[...] = jnp.where((ox == src[0, 0]) & (oy == src[0, 1]) & (oz == src[0, 2]), 1.0, 0.0).astype(f32)
    live = mask[...].astype(f32)
    T[...] = jnp.zeros_like(T)
    for t in range(STEPS):
        T[t, :, 0:NB * bx] = (live * rec[t]).T
    surface = lax.broadcasted_iota(jnp.int32, (bys, bz), 1) == 0

    W[R * bx:(R + 1) * bx] = vel[...]

    def laplace(field, t, b):
        own = at(field, t, b)
        flat = own.reshape(bx * bys, bz)
        high = flat.astype(bf16)
        low = (flat - high.astype(f32)).astype(bf16)
        both = jnp.concatenate([high, low], axis=1)
        prod = jnp.dot(both, B[...], preferred_element_type=f32)
        total = (prod[:, :bz] + prod[:, bz:]).reshape(bx, bys, bz)
        for j in range(1, 5):
            near_sum = (field[t, pl.ds(4 + j + b * bx, bx), 8:16, :] + field[t, pl.ds(4 - j + b * bx, bx), 8:16, :]
                        + field[t, pl.ds(4 + b * bx, bx), 8 + j:16 + j, :] + field[t, pl.ds(4 + b * bx, bx), 8 - j:16 - j, :])
            total = total + coeffs[j] * near_sum
        return own, total

    def source_term(step, b):
        amp = jnp.where(b == R, wav[0, step], 0.0)
        return amp * O[...]

    def receiver_term(step, b):
        row = pltpu.roll(T[STEPS - 1 - step], 128 - b * bx, 1) * keep_of(b)
        parts = []
        for x in range(bx):
            moved = pltpu.roll(row, 128 - x, 1) if x else row
            parts.append(jnp.where(surface, moved, 0.0)[None])
        return jnp.concatenate(parts, axis=0)

    rim_copy(F, 0, fs, fr).wait_recv()
    rim_copy(A, 0, as_, ar).wait_recv()

    def first_diff(b, c):
        cells = pl.ds(b * bx, bx)
        ZF[cells] = laplace(F, 0, b)[1]
        ZA[cells] = laplace(A, 0, b)[1]
        return c

    lax.fori_loop(lo, hi, first_diff, 0)
    for o in offsets:
        @pl.when(near(o))
        def _():
            vel_copy(-o).wait_recv()

    def first_f(b, c):
        kb = keep_of(b)
        cells = pl.ds(b * bx, bx)
        w = kb * W[cells]
        W[cells] = w
        F[1, pl.ds(4 + b * bx, bx), 8:16, :] = (
            2.0 * at(F, 0, b) - kb * fwd[0, cells].astype(f32) + w * ZF[cells] + source_term(0, b))
        return c

    lax.fori_loop(lo, hi, first_f, 0)
    rim_copy(F, 1, fs, fr).start()

    def first_a(b, c):
        cells = pl.ds(b * bx, bx)
        A[1, pl.ds(4 + b * bx, bx), 8:16, :] = (
            2.0 * at(A, 0, b) - keep_of(b) * adj[0, cells].astype(f32) + W[cells] * ZA[cells] + receiver_term(0, b))
        return c

    lax.fori_loop(lo, hi, first_a, 0)
    rim_copy(A, 1, as_, ar).start()

    def image_copy(j):
        return pltpu.make_async_remote_copy(
            src_ref=PV.at[pl.ds(j * bx, bx)], dst_ref=G.at[j], send_sem=gs.at[j], recv_sem=gr.at[j],
            device_id={"block": home + j - R}, device_id_type=MESH)

    for step in range(1, STEPS):
        last = step == STEPS - 1
        rim_copy(F, step, fs, fr).wait_recv()

        def f_block(b, c):
            cells = pl.ds(b * bx, bx)
            own, lap = laplace(F, step, b)
            new = 2.0 * own - at(F, step - 1, b) + W[cells] * lap + source_term(step, b)
            if not last:
                F[step + 1, pl.ds(4 + b * bx, bx), 8:16, :] = new
            if step + 1 > 2:
                PV[cells] = PV[cells] + new * at(A, STEPS - step - 1, b)
            return c

        lax.fori_loop(lo, hi, f_block, 0)
        if not last:
            rim_copy(F, step + 1, fs, fr).start()
        rim_copy(A, step, as_, ar).wait_recv()

        def a_block(b, c):
            cells = pl.ds(b * bx, bx)
            own, lap = laplace(A, step, b)
            new = 2.0 * own - at(A, step - 1, b) + W[cells] * lap + receiver_term(step, b)
            if not last:
                A[step + 1, pl.ds(4 + b * bx, bx), 8:16, :] = new
            if step == 1:
                PV[cells] = at(F, 2, b) * new
            else:
                PV[cells] = PV[cells] + at(F, STEPS - step - 1, b) * new
            if last:
                @pl.when(b != R)
                def _():
                    image_copy(b).start()
            return c

        lax.fori_loop(lo, hi, a_block, 0)
        if not last:
            rim_copy(A, step + 1, as_, ar).start()

    H[...] = PV[R * bx:(R + 1) * bx]
    for o in (-1, 1, -2, 2):
        @pl.when(near(o))
        def _():
            j = R - o
            image_copy(j).wait_recv()
            H[...] = H[...] + G[j]

    zl = bz // nshot
    xg = bx // nshot
    lane = lax.broadcasted_iota(jnp.int32, (xg, bys, bz), 2)

    def packed(d):
        total = jnp.zeros((xg, bys, bz), f32)
        for k in range(nshot):
            shift = lax.rem((k - d + nshot) * zl, bz)
            moved = pltpu.roll(H[k * xg:(k + 1) * xg].reshape(xg * bys, bz), shift, 1).reshape(xg, bys, bz)
            total = jnp.where((lane >= k * zl) & (lane < (k + 1) * zl), moved, total)
        return total

    def team_copy(r):
        return pltpu.make_async_remote_copy(
            src_ref=S.at[r], dst_ref=S.at[nshot + r], send_sem=ss.at[r], recv_sem=sr.at[r],
            device_id={"shot": lax.rem(team + r, nshot)}, device_id_type=MESH)

    for r in range(1, nshot):
        S[r] = packed(lax.rem(team + r, nshot))
        team_copy(r).start()
    total = packed(team)
    for r in range(1, nshot):
        team_copy(r).wait_recv()
        total = total + S[nshot + r]
    out[...] = image_scale * total

    for t in range(STEPS):
        rim_copy(F, t, fs, fr).wait_send()
        rim_copy(A, t, as_, ar).wait_send()
    for o in offsets:
        @pl.when(near(o))
        def _():
            vel_copy(o).wait_send()
            image_copy(R + o).wait_send()
    for r in range(1, nshot):
        team_copy(r).wait_send()


def clear_at(F, A, row, bx, bz, b, c):
    for field in (F, A):
        for t in range(STEPS):
            field[t, pl.ds(4 + b * bx, bx), row:row + 8, :] = jnp.zeros((bx, 8, bz), f32)
    return c


def shards(nblock, nshot, vel_sq, fwd_state, adj_state, wavelet, source, aperture, rec_mask, rec_data):
    bx, bys, bz = vel_sq.shape[1:]
    width = NB * bx
    vmem = pl.BlockSpec(memory_space=pltpu.VMEM)
    smem = pl.BlockSpec(memory_space=pltpu.SMEM)
    dma = pltpu.SemaphoreType.DMA
    packed = pl.pallas_call(
        functools.partial(kernel, nblock, nshot),
        out_shape=jax.ShapeDtypeStruct((bx // nshot, bys, bz), f32),
        in_specs=[vmem, vmem, vmem, smem, smem, smem, vmem, vmem],
        out_specs=vmem,
        scratch_shapes=[
            pltpu.VMEM((STEPS, width + 8, 24, bz), f32),
            pltpu.VMEM((STEPS, width + 8, 24, bz), f32),
            pltpu.VMEM((width, bys, bz), f32),
            pltpu.VMEM((width, bys, bz), f32),
            pltpu.VMEM((width, bys, bz), f32),
            pltpu.VMEM((width, bys, bz), f32),
            pltpu.VMEM((bx, bys, bz), f32),
            pltpu.VMEM((STEPS, bys, bz), f32),
            pltpu.VMEM((2 * bz, 2 * bz), bf16),
            pltpu.VMEM((NB, bx, bys, bz), f32),
            pltpu.VMEM((2 * nshot, bx // nshot, bys, bz), f32),
            pltpu.VMEM((bx, bys, bz), f32),
            dma((NB,)), dma((NB,)),
            dma((STEPS,)), dma((STEPS,)),
            dma((STEPS,)), dma((STEPS,)),
            dma((NB,)), dma((NB,)),
            dma((nshot,)), dma((nshot,)),
        ],
        compiler_params=pltpu.CompilerParams(
            collective_id=0, has_side_effects=True, vmem_limit_bytes=40 * 1024 * 1024),
    )(vel_sq[0], fwd_state[0], adj_state[0], wavelet, source, aperture, rec_mask[0], rec_data[0])
    zl = bz // nshot
    image = packed.reshape(bx // nshot, bys, nshot, zl).transpose(2, 0, 1, 3)
    return image.reshape(1, bx, bys, zl)


def solution(mesh):
    placed = (
        P(("parts", "block"), None, "sub", None),
        P(("parts", "block", "shot"), None, None, "sub", None),
        P(("parts", "block", "shot"), None, None, "sub", None),
        P(("parts", "block", "shot"), None),
        P(("parts", "block", "shot"), None),
        P(("parts", "block", "shot"), None),
        P(("parts", "block", "shot"), None, "sub"),
        P(("parts", "block", "shot"), None, None, "sub"),
    )
    return jax.shard_map(
        functools.partial(shards, mesh.shape["block"], mesh.shape["shot"]),
        mesh=mesh,
        in_specs=placed,
        out_specs=P(("parts", "block"), None, "sub", "shot"),
        check_vma=False,
    )
```

```python
import functools

import jax
import jax.numpy as jnp
from jax import lax
from jax.experimental import pallas as pl
from jax.experimental.pallas import tpu as pltpu
from jax.sharding import PartitionSpec as P

R = 2
STEPS = 4
NB = 2 * R + 1
MESH = pl.DeviceIdType.MESH

coeffs = (-205.0 / 72.0, 8.0 / 5.0, -1.0 / 5.0, 8.0 / 315.0, -1.0 / 560.0)
image_scale = 0.05
f32 = jnp.float32
bf16 = jnp.bfloat16


def kernel(nblock, nshot, vel, fwd, adj, wav, src, ap, mask, rec, out,
           F, A, W, ZF, ZA, PV, O, T, B, G, S, H, FI, AI, RI, MI,
           ls, vs, vr, fs, fr, as_, ar, gs, gr, ss, sr):
    bx, bys, bz = vel.shape
    home = lax.axis_index("block")
    team = lax.axis_index("shot")
    sub = lax.axis_index("sub")
    lo = jnp.maximum(R - home, 0)
    hi = jnp.minimum(R + nblock - home, NB)
    n = hi - lo
    offsets = [o for o in range(-R, R + 1) if o != 0]
    down = (2 * home < nblock).astype(jnp.int32)
    first = down * (hi - 1) + (1 - down) * lo
    turn = 1 - 2 * down

    def near(o):
        return (home + o >= 0) & (home + o < nblock)

    barrier = pltpu.get_barrier_semaphore()
    for o in offsets:
        @pl.when(near(o))
        def _():
            pl.semaphore_signal(barrier, inc=1, device_id={"block": home + o}, device_id_type=MESH)
    for r in range(1, nshot):
        pl.semaphore_signal(barrier, inc=1, device_id={"shot": lax.rem(team + r, nshot)}, device_id_type=MESH)
    pl.semaphore_signal(barrier, inc=1, device_id={"sub": 1 - sub}, device_id_type=MESH)

    local = [pltpu.make_async_copy(fwd, FI, ls.at[0]), pltpu.make_async_copy(adj, AI, ls.at[1]),
             pltpu.make_async_copy(rec, RI, ls.at[2]), pltpu.make_async_copy(mask, MI, ls.at[3]),
             pltpu.make_async_copy(vel, W.at[pl.ds(R * bx, bx)], ls.at[4])]
    for copy in local:
        copy.start()

    def keep_of(b):
        return jnp.where((b >= R - ap[0, 0]) & (b <= R + ap[0, 1]), 1.0, 0.0).astype(f32)

    def at(field, t, b):
        return field[t, pl.ds(4 + b * bx, bx), 8:16, :]

    def state(ref, t, b):
        rows = pl.ds(pl.multiple_of(t * NB * bx * bys + b * bx * bys, bx * bys), bx * bys)
        return ref[rows, :].astype(f32).reshape(bx, bys, bz)

    zx = jnp.zeros((4, 8, bz), f32)

    @pl.when(sub == 0)
    def _():
        lax.fori_loop(lo, hi, functools.partial(clear_at, F, A, 0, bx, bz), 0)

    @pl.when(sub == 1)
    def _():
        lax.fori_loop(lo, hi, functools.partial(clear_at, F, A, 16, bx, bz), 0)

    for field in (F, A):
        for t in range(STEPS):
            field[t, pl.ds(lo * bx, 4), 8:16, :] = zx
            field[t, pl.ds(4 + hi * bx, 4), 8:16, :] = zx

    pl.semaphore_wait(barrier, (n - 1) + (nshot - 1) + 1)

    def vel_copy(o):
        j = R - o
        return pltpu.make_async_remote_copy(
            src_ref=vel, dst_ref=W.at[pl.ds(j * bx, bx)], send_sem=vs.at[j], recv_sem=vr.at[j],
            device_id={"block": home + o}, device_id_type=MESH)

    for o in (-2, 2, -1, 1):
        @pl.when(near(o))
        def _():
            vel_copy(o).start()

    def rim(side, field, t, b, ssem, rsem):
        x = pl.ds(4 + b * bx, bx)
        return pltpu.make_async_remote_copy(
            src_ref=field.at[t, x, pl.ds(8 if side else 12, 4), :],
            dst_ref=field.at[t, x, pl.ds(16 if side else 4, 4), :],
            send_sem=ssem.at[t, b], recv_sem=rsem.at[t, b],
            device_id={"sub": 1 - sub}, device_id_type=MESH)

    def rim_start(t, b):
        for side in range(2):
            @pl.when(sub == side)
            def _():
                rim(side, F, t, b, fs, fr).start()
                rim(side, A, t, b, as_, ar).start()

    def rim_wait(t, b):
        for side in range(2):
            @pl.when(sub == side)
            def _():
                rim(1 - side, F, t, b, fs, fr).wait_recv()
                rim(1 - side, A, t, b, as_, ar).wait_recv()

    def rim_sent(t, b):
        for side in range(2):
            @pl.when(sub == side)
            def _():
                rim(side, F, t, b, fs, fr).wait_send()
                rim(side, A, t, b, as_, ar).wait_send()

    local[0].wait()
    local[1].wait()

    def load_states(i, c):
        b = first + turn * i
        kb = keep_of(b)
        rows = pl.ds(4 + b * bx, bx)
        F[0, rows, 8:16, :] = kb * state(FI, 1, b)
        A[0, rows, 8:16, :] = kb * state(AI, 1, b)
        rim_start(0, b)
        return c

    lax.fori_loop(0, n, load_states, 0)

    i0 = lax.broadcasted_iota(jnp.int32, (bz, bz), 0)
    i1 = lax.broadcasted_iota(jnp.int32, (bz, bz), 1)
    dist = jnp.abs(i0 - i1)
    band = jnp.where(dist == 0, 3.0 * coeffs[0], 0.0).astype(f32)
    for j in range(1, 5):
        band = jnp.where(dist == j, coeffs[j], band)
    band_hi = band.astype(bf16)
    band_lo = (band - band_hi.astype(f32)).astype(bf16)
    B[0:bz, 0:bz] = band_hi
    B[bz:2 * bz, 0:bz] = band_hi
    B[0:bz, bz:2 * bz] = band_lo
    B[bz:2 * bz, bz:2 * bz] = jnp.zeros((bz, bz), bf16)

    ox = lax.broadcasted_iota(jnp.int32, (bx, bys, bz), 0)
    oy = lax.broadcasted_iota(jnp.int32, (bx, bys, bz), 1) + sub * bys
    oz = lax.broadcasted_iota(jnp.int32, (bx, bys, bz), 2)
    O[...] = jnp.where((ox == src[0, 0]) & (oy == src[0, 1]) & (oz == src[0, 2]), 1.0, 0.0).astype(f32)
    local[2].wait()
    local[3].wait()
    local[4].wait()
    live = MI[...].astype(f32)
    T[...] = jnp.zeros_like(T)
    for t in range(STEPS):
        T[t, :, 0:NB * bx] = live * RI[t]
    surface = lax.broadcasted_iota(jnp.int32, (bys, bz), 1) == 0

    def laplace(t, b):
        flat = jnp.concatenate([at(F, t, b).reshape(bx * bys, bz), at(A, t, b).reshape(bx * bys, bz)], axis=0)
        high = flat.astype(bf16)
        low = (flat - high.astype(f32)).astype(bf16)
        both = jnp.concatenate([high, low], axis=1)
        prod = jnp.dot(both, B[...], preferred_element_type=f32)
        depth = prod[:, :bz] + prod[:, bz:]
        result = []
        for k, field in enumerate((F, A)):
            total = depth[k * bx * bys:(k + 1) * bx * bys].reshape(bx, bys, bz)
            for j in range(1, 5):
                total = total + coeffs[j] * (
                    field[t, pl.ds(4 + j + b * bx, bx), 8:16, :] + field[t, pl.ds(4 - j + b * bx, bx), 8:16, :]
                    + field[t, pl.ds(4 + b * bx, bx), 8 + j:16 + j, :] + field[t, pl.ds(4 + b * bx, bx), 8 - j:16 - j, :])
            result.append(total)
        return result

    def source_term(step, b):
        return jnp.where(b == R, wav[0, step], 0.0) * O[...]

    def receiver_term(step, b):
        row = pltpu.roll(T[STEPS - 1 - step], 128 - b * bx, 1) * keep_of(b)
        parts = []
        for x in range(bx):
            moved = pltpu.roll(row, 128 - x, 1) if x else row
            parts.append(jnp.where(surface, moved, 0.0)[None])
        return jnp.concatenate(parts, axis=0)

    def first_diff(i, c):
        b = first + turn * i
        rim_wait(0, b)
        cells = pl.ds(b * bx, bx)
        ZF[cells], ZA[cells] = laplace(0, b)
        return c

    lax.fori_loop(0, n, first_diff, 0)

    def image_copy(j):
        return pltpu.make_async_remote_copy(
            src_ref=PV.at[pl.ds(j * bx, bx)], dst_ref=G.at[j], send_sem=gs.at[j], recv_sem=gr.at[j],
            device_id={"block": home + j - R}, device_id_type=MESH)

    def vel_wait(b):
        pltpu.make_async_remote_copy(
            src_ref=vel, dst_ref=W.at[pl.ds(b * bx, bx)], send_sem=vs.at[b], recv_sem=vr.at[b],
            device_id={"block": home + b - R}, device_id_type=MESH).wait_recv()

    def advance(step, b):
        last = step == STEPS - 1
        cells = pl.ds(b * bx, bx)
        if step == 0:
            @pl.when(b != R)
            def _():
                vel_wait(b)
            kb = keep_of(b)
            w = kb * W[cells]
            W[cells] = w
            lap_f, lap_a = ZF[cells], ZA[cells]
            old_f, old_a = kb * state(FI, 0, b), kb * state(AI, 0, b)
        else:
            rim_wait(step, b)
            w = W[cells]
            lap_f, lap_a = laplace(step, b)
            old_f, old_a = at(F, step - 1, b), at(A, step - 1, b)
        new_f = 2.0 * at(F, step, b) - old_f + w * lap_f + source_term(step, b)
        new_a = 2.0 * at(A, step, b) - old_a + w * lap_a + receiver_term(step, b)
        if not last:
            F[step + 1, pl.ds(4 + b * bx, bx), 8:16, :] = new_f
            A[step + 1, pl.ds(4 + b * bx, bx), 8:16, :] = new_a
            rim_start(step + 1, b)
        if step == 1:
            PV[cells] = new_f * new_a
        elif step > 1:
            early = STEPS - 1 - step
            PV[cells] = PV[cells] + new_f * at(A, early, b) + at(F, early, b) * new_a
        if last:
            @pl.when(b != R)
            def _():
                image_copy(b).start()

    def wave(k, c):
        for step in range(STEPS):
            @pl.when((k >= step) & (k - step < n))
            def _():
                advance(step, first + turn * (k - step))
        return c

    lax.fori_loop(0, n + STEPS - 1, wave, 0)

    H[...] = PV[R * bx:(R + 1) * bx]
    for o in (-1, 1, -2, 2):
        @pl.when(near(o))
        def _():
            j = R - o
            image_copy(j).wait_recv()
            H[...] = H[...] + G[j]

    zl = bz // nshot
    xg = bx // nshot
    lane = lax.broadcasted_iota(jnp.int32, (xg, bys, bz), 2)

    def packed(d):
        total = jnp.zeros((xg, bys, bz), f32)
        for k in range(nshot):
            shift = lax.rem((k - d + nshot) * zl, bz)
            moved = pltpu.roll(H[k * xg:(k + 1) * xg].reshape(xg * bys, bz), shift, 1).reshape(xg, bys, bz)
            total = jnp.where((lane >= k * zl) & (lane < (k + 1) * zl), moved, total)
        return total

    def team_copy(r):
        return pltpu.make_async_remote_copy(
            src_ref=S.at[r], dst_ref=S.at[nshot + r], send_sem=ss.at[r], recv_sem=sr.at[r],
            device_id={"shot": lax.rem(team + r, nshot)}, device_id_type=MESH)

    for r in range(1, nshot):
        S[r] = packed(lax.rem(team + r, nshot))
        team_copy(r).start()
    total = packed(team)
    for r in range(1, nshot):
        team_copy(r).wait_recv()
        total = total + S[nshot + r]
    out[...] = image_scale * total

    def sent(b, c):
        for t in range(STEPS):
            rim_sent(t, b)
        return c

    lax.fori_loop(lo, hi, sent, 0)
    for o in offsets:
        @pl.when(near(o))
        def _():
            vel_copy(o).wait_send()
            image_copy(R + o).wait_send()
    for r in range(1, nshot):
        team_copy(r).wait_send()


def clear_at(F, A, row, bx, bz, b, c):
    for field in (F, A):
        for t in range(STEPS):
            field[t, pl.ds(4 + b * bx, bx), row:row + 8, :] = jnp.zeros((bx, 8, bz), f32)
    return c


def shards(nblock, nshot, vel_sq, fwd_state, adj_state, wavelet, source, aperture, rec_mask, rec_data):
    bx, bys, bz = vel_sq.shape[1:]
    width = NB * bx
    vmem = pl.BlockSpec(memory_space=pltpu.VMEM)
    hbm = pl.BlockSpec(memory_space=pltpu.HBM)
    smem = pl.BlockSpec(memory_space=pltpu.SMEM)
    dma = pltpu.SemaphoreType.DMA
    packed = pl.pallas_call(
        functools.partial(kernel, nblock, nshot),
        out_shape=jax.ShapeDtypeStruct((bx // nshot, bys, bz), f32),
        in_specs=[hbm, hbm, hbm, smem, smem, smem, hbm, hbm],
        out_specs=vmem,
        scratch_shapes=[
            pltpu.VMEM((STEPS, width + 8, 24, bz), f32),
            pltpu.VMEM((STEPS, width + 8, 24, bz), f32),
            pltpu.VMEM((width, bys, bz), f32),
            pltpu.VMEM((width, bys, bz), f32),
            pltpu.VMEM((width, bys, bz), f32),
            pltpu.VMEM((width, bys, bz), f32),
            pltpu.VMEM((bx, bys, bz), f32),
            pltpu.VMEM((STEPS, bys, bz), f32),
            pltpu.VMEM((2 * bz, 2 * bz), bf16),
            pltpu.VMEM((NB, bx, bys, bz), f32),
            pltpu.VMEM((2 * nshot, bx // nshot, bys, bz), f32),
            pltpu.VMEM((bx, bys, bz), f32),
            pltpu.VMEM((2 * width * bys, bz), bf16),
            pltpu.VMEM((2 * width * bys, bz), bf16),
            pltpu.VMEM((STEPS, bys, width), f32),
            pltpu.VMEM((bys, width), jnp.int32),
            dma((5,)),
            dma((NB,)), dma((NB,)),
            dma((STEPS, NB)), dma((STEPS, NB)),
            dma((STEPS, NB)), dma((STEPS, NB)),
            dma((NB,)), dma((NB,)),
            dma((nshot,)), dma((nshot,)),
        ],
        compiler_params=pltpu.CompilerParams(
            collective_id=0, has_side_effects=True, vmem_limit_bytes=63 * 1024 * 1024),
    )(vel_sq[0], fwd_state.reshape(-1, bz), adj_state.reshape(-1, bz), wavelet, source, aperture,
      rec_mask[0].T, rec_data[0].transpose(0, 2, 1))
    zl = bz // nshot
    image = packed.reshape(bx // nshot, bys, nshot, zl).transpose(2, 0, 1, 3)
    return image.reshape(1, bx, bys, zl)


def solution(mesh):
    placed = (
        P(("parts", "block"), None, "sub", None),
        P(("parts", "block", "shot"), None, None, "sub", None),
        P(("parts", "block", "shot"), None, None, "sub", None),
        P(("parts", "block", "shot"), None),
        P(("parts", "block", "shot"), None),
        P(("parts", "block", "shot"), None),
        P(("parts", "block", "shot"), None, "sub"),
        P(("parts", "block", "shot"), None, None, "sub"),
    )
    return jax.shard_map(
        functools.partial(shards, mesh.shape["block"], mesh.shape["shot"]),
        mesh=mesh,
        in_specs=placed,
        out_specs=P(("parts", "block"), None, "sub", "shot"),
        check_vma=False,
    )
```

```python
import functools

import jax
import jax.numpy as jnp
from jax import lax
from jax.experimental import pallas as pl
from jax.experimental.pallas import tpu as pltpu
from jax.sharding import PartitionSpec as P

R = 2
STEPS = 4
NB = 2 * R + 1
MESH = pl.DeviceIdType.MESH

coeffs = (-205.0 / 72.0, 8.0 / 5.0, -1.0 / 5.0, 8.0 / 315.0, -1.0 / 560.0)
image_scale = 0.05
vel_mid = 0.12
vel_step = 0.06 / 32000.0
f32 = jnp.float32
bf16 = jnp.bfloat16


def kernel(nblock, nshot, vel, fwd, adj, wav, src, ap, mask, rec, out,
           F, A, W, ZF, ZA, PV, O, T, B, G, S, H, FI, AI, RI, MI, VC, VG,
           ls, vs, vr, fs, fr, as_, ar, gs, gr, ss, sr):
    bx, bys, bz = vel.shape
    home = lax.axis_index("block")
    team = lax.axis_index("shot")
    sub = lax.axis_index("sub")
    lo = jnp.maximum(R - home, 0)
    hi = jnp.minimum(R + nblock - home, NB)
    n = hi - lo
    offsets = [o for o in range(-R, R + 1) if o != 0]
    down = (2 * home < nblock).astype(jnp.int32)
    first = down * (hi - 1) + (1 - down) * lo
    turn = 1 - 2 * down

    def near(o):
        return (home + o >= 0) & (home + o < nblock)

    barrier = pltpu.get_barrier_semaphore()
    for o in offsets:
        @pl.when(near(o))
        def _():
            pl.semaphore_signal(barrier, inc=1, device_id={"block": home + o}, device_id_type=MESH)
    for r in range(1, nshot):
        pl.semaphore_signal(barrier, inc=1, device_id={"shot": lax.rem(team + r, nshot)}, device_id_type=MESH)
    pl.semaphore_signal(barrier, inc=1, device_id={"sub": 1 - sub}, device_id_type=MESH)

    local = [pltpu.make_async_copy(fwd, FI, ls.at[0]), pltpu.make_async_copy(adj, AI, ls.at[1]),
             pltpu.make_async_copy(rec, RI, ls.at[2]), pltpu.make_async_copy(mask, MI, ls.at[3]),
             pltpu.make_async_copy(vel, W.at[pl.ds(R * bx, bx)], ls.at[4])]
    for copy in local[::-1]:
        copy.start()

    def keep_of(b):
        return jnp.where((b >= R - ap[0, 0]) & (b <= R + ap[0, 1]), 1.0, 0.0).astype(f32)

    def at(field, t, b):
        return field[t, pl.ds(4 + b * bx, bx), 8:16, :]

    def state(ref, t, b):
        rows = pl.ds(pl.multiple_of(t * NB * bx * bys + b * bx * bys, bx * bys), bx * bys)
        return ref[rows, :].astype(f32).reshape(bx, bys, bz)

    zx = jnp.zeros((4, 8, bz), f32)

    @pl.when(sub == 0)
    def _():
        lax.fori_loop(lo, hi, functools.partial(clear_at, F, A, 0, bx, bz), 0)

    @pl.when(sub == 1)
    def _():
        lax.fori_loop(lo, hi, functools.partial(clear_at, F, A, 16, bx, bz), 0)

    for field in (F, A):
        for t in range(STEPS):
            field[t, pl.ds(lo * bx, 4), 8:16, :] = zx
            field[t, pl.ds(4 + hi * bx, 4), 8:16, :] = zx

    local[4].wait()
    code = jnp.round((W[R * bx:(R + 1) * bx].reshape(bx * bys, bz) - vel_mid) * (1.0 / vel_step))
    VC[...] = code.astype(jnp.int32).astype(jnp.int16)

    pl.semaphore_wait(barrier, (n - 1) + (nshot - 1) + 1)

    def vel_copy(o):
        j = R - o
        return pltpu.make_async_remote_copy(
            src_ref=VC, dst_ref=VG.at[j], send_sem=vs.at[j], recv_sem=vr.at[j],
            device_id={"block": home + o}, device_id_type=MESH)

    for o in (-2, 2, -1, 1):
        @pl.when(near(o))
        def _():
            vel_copy(o).start()

    def rim(side, field, t, b, ssem, rsem):
        x = pl.ds(4 + b * bx, bx)
        return pltpu.make_async_remote_copy(
            src_ref=field.at[t, x, pl.ds(8 if side else 12, 4), :],
            dst_ref=field.at[t, x, pl.ds(16 if side else 4, 4), :],
            send_sem=ssem.at[t, b], recv_sem=rsem.at[t, b],
            device_id={"sub": 1 - sub}, device_id_type=MESH)

    def rim_start(t, b):
        for side in range(2):
            @pl.when(sub == side)
            def _():
                rim(side, F, t, b, fs, fr).start()
                rim(side, A, t, b, as_, ar).start()

    def rim_wait(t, b):
        for side in range(2):
            @pl.when(sub == side)
            def _():
                rim(1 - side, F, t, b, fs, fr).wait_recv()
                rim(1 - side, A, t, b, as_, ar).wait_recv()

    def rim_sent(t, b):
        for side in range(2):
            @pl.when(sub == side)
            def _():
                rim(side, F, t, b, fs, fr).wait_send()
                rim(side, A, t, b, as_, ar).wait_send()

    local[0].wait()
    local[1].wait()

    def load_states(i, c):
        b = first + turn * i
        kb = keep_of(b)
        rows = pl.ds(4 + b * bx, bx)
        F[0, rows, 8:16, :] = kb * state(FI, 1, b)
        A[0, rows, 8:16, :] = kb * state(AI, 1, b)
        rim_start(0, b)
        return c

    lax.fori_loop(0, n, load_states, 0)

    i0 = lax.broadcasted_iota(jnp.int32, (bz, bz), 0)
    i1 = lax.broadcasted_iota(jnp.int32, (bz, bz), 1)
    dist = jnp.abs(i0 - i1)
    band = jnp.where(dist == 0, 3.0 * coeffs[0], 0.0).astype(f32)
    for j in range(1, 5):
        band = jnp.where(dist == j, coeffs[j], band)
    band_hi = band.astype(bf16)
    band_lo = (band - band_hi.astype(f32)).astype(bf16)
    B[0:bz, 0:bz] = band_hi
    B[bz:2 * bz, 0:bz] = band_hi
    B[0:bz, bz:2 * bz] = band_lo
    B[bz:2 * bz, bz:2 * bz] = jnp.zeros((bz, bz), bf16)

    ox = lax.broadcasted_iota(jnp.int32, (bx, bys, bz), 0)
    oy = lax.broadcasted_iota(jnp.int32, (bx, bys, bz), 1) + sub * bys
    oz = lax.broadcasted_iota(jnp.int32, (bx, bys, bz), 2)
    O[...] = jnp.where((ox == src[0, 0]) & (oy == src[0, 1]) & (oz == src[0, 2]), 1.0, 0.0).astype(f32)
    local[2].wait()
    local[3].wait()
    live = MI[...].astype(f32)
    T[...] = jnp.zeros_like(T)
    for t in range(STEPS):
        T[t, :, 0:NB * bx] = live * RI[t]
    surface = lax.broadcasted_iota(jnp.int32, (bys, bz), 1) == 0

    def laplace(t, b):
        flat = jnp.concatenate([at(F, t, b).reshape(bx * bys, bz), at(A, t, b).reshape(bx * bys, bz)], axis=0)
        high = flat.astype(bf16)
        low = (flat - high.astype(f32)).astype(bf16)
        both = jnp.concatenate([high, low], axis=1)
        prod = jnp.dot(both, B[...], preferred_element_type=f32)
        depth = prod[:, :bz] + prod[:, bz:]
        result = []
        for k, field in enumerate((F, A)):
            total = depth[k * bx * bys:(k + 1) * bx * bys].reshape(bx, bys, bz)
            for j in range(1, 5):
                total = total + coeffs[j] * (
                    field[t, pl.ds(4 + j + b * bx, bx), 8:16, :] + field[t, pl.ds(4 - j + b * bx, bx), 8:16, :]
                    + field[t, pl.ds(4 + b * bx, bx), 8 + j:16 + j, :] + field[t, pl.ds(4 + b * bx, bx), 8 - j:16 - j, :])
            result.append(total)
        return result

    def source_term(step, b):
        return jnp.where(b == R, wav[0, step], 0.0) * O[...]

    def receiver_term(step, b):
        row = pltpu.roll(T[STEPS - 1 - step], 128 - b * bx, 1) * keep_of(b)
        parts = []
        for x in range(bx):
            moved = pltpu.roll(row, 128 - x, 1) if x else row
            parts.append(jnp.where(surface, moved, 0.0)[None])
        return jnp.concatenate(parts, axis=0)

    def first_diff(i, c):
        b = first + turn * i
        rim_wait(0, b)
        cells = pl.ds(b * bx, bx)
        ZF[cells], ZA[cells] = laplace(0, b)
        return c

    lax.fori_loop(0, n, first_diff, 0)

    def image_copy(j):
        return pltpu.make_async_remote_copy(
            src_ref=PV.at[pl.ds(j * bx, bx)], dst_ref=G.at[j], send_sem=gs.at[j], recv_sem=gr.at[j],
            device_id={"block": home + j - R}, device_id_type=MESH)

    def vel_wait(b):
        pltpu.make_async_remote_copy(
            src_ref=VC, dst_ref=VG.at[b], send_sem=vs.at[b], recv_sem=vr.at[b],
            device_id={"block": home + b - R}, device_id_type=MESH).wait_recv()

    def advance(step, b):
        last = step == STEPS - 1
        cells = pl.ds(b * bx, bx)
        if step == 0:
            @pl.when(b != R)
            def _():
                vel_wait(b)
                W[cells] = (VG[b].astype(jnp.int32).astype(f32) * vel_step + vel_mid).reshape(bx, bys, bz)
            kb = keep_of(b)
            w = kb * W[cells]
            W[cells] = w
            lap_f, lap_a = ZF[cells], ZA[cells]
            old_f, old_a = kb * state(FI, 0, b), kb * state(AI, 0, b)
        else:
            rim_wait(step, b)
            w = W[cells]
            lap_f, lap_a = laplace(step, b)
            old_f, old_a = at(F, step - 1, b), at(A, step - 1, b)
        new_f = 2.0 * at(F, step, b) - old_f + w * lap_f + source_term(step, b)
        new_a = 2.0 * at(A, step, b) - old_a + w * lap_a + receiver_term(step, b)
        if not last:
            F[step + 1, pl.ds(4 + b * bx, bx), 8:16, :] = new_f
            A[step + 1, pl.ds(4 + b * bx, bx), 8:16, :] = new_a
            rim_start(step + 1, b)
        if step == 1:
            PV[cells] = new_f * new_a
        elif step > 1:
            early = STEPS - 1 - step
            PV[cells] = PV[cells] + new_f * at(A, early, b) + at(F, early, b) * new_a
        if last:
            @pl.when(b != R)
            def _():
                image_copy(b).start()

    def wave(k, c):
        for step in range(STEPS):
            @pl.when((k >= step) & (k - step < n))
            def _():
                advance(step, first + turn * (k - step))
        return c

    lax.fori_loop(0, n + STEPS - 1, wave, 0)

    H[...] = PV[R * bx:(R + 1) * bx]
    for o in (-1, 1, -2, 2):
        @pl.when(near(o))
        def _():
            j = R - o
            image_copy(j).wait_recv()
            H[...] = H[...] + G[j]

    zl = bz // nshot
    xg = bx // nshot
    lane = lax.broadcasted_iota(jnp.int32, (xg, bys, bz), 2)

    def packed(d):
        total = jnp.zeros((xg, bys, bz), f32)
        for k in range(nshot):
            shift = lax.rem((k - d + nshot) * zl, bz)
            moved = pltpu.roll(H[k * xg:(k + 1) * xg].reshape(xg * bys, bz), shift, 1).reshape(xg, bys, bz)
            total = jnp.where((lane >= k * zl) & (lane < (k + 1) * zl), moved, total)
        return total

    def team_copy(r):
        return pltpu.make_async_remote_copy(
            src_ref=S.at[r], dst_ref=S.at[nshot + r], send_sem=ss.at[r], recv_sem=sr.at[r],
            device_id={"shot": lax.rem(team + r, nshot)}, device_id_type=MESH)

    for r in range(1, nshot):
        S[r] = packed(lax.rem(team + r, nshot))
        team_copy(r).start()
    total = packed(team)
    for r in range(1, nshot):
        team_copy(r).wait_recv()
        total = total + S[nshot + r]
    total = image_scale * total
    for k in range(nshot):
        flat = total.reshape(xg * bys, bz)
        moved = pltpu.roll(flat, bz - k * zl, 1) if k else flat
        out[k * xg:(k + 1) * xg] = moved.reshape(xg, bys, bz)[:, :, :zl]

    def sent(b, c):
        for t in range(STEPS):
            rim_sent(t, b)
        return c

    lax.fori_loop(lo, hi, sent, 0)
    for o in offsets:
        @pl.when(near(o))
        def _():
            vel_copy(o).wait_send()
            image_copy(R + o).wait_send()
    for r in range(1, nshot):
        team_copy(r).wait_send()


def clear_at(F, A, row, bx, bz, b, c):
    for field in (F, A):
        for t in range(STEPS):
            field[t, pl.ds(4 + b * bx, bx), row:row + 8, :] = jnp.zeros((bx, 8, bz), f32)
    return c


def shards(nblock, nshot, vel_sq, fwd_state, adj_state, wavelet, source, aperture, rec_mask, rec_data):
    bx, bys, bz = vel_sq.shape[1:]
    width = NB * bx
    vmem = pl.BlockSpec(memory_space=pltpu.VMEM)
    hbm = pl.BlockSpec(memory_space=pltpu.HBM)
    smem = pl.BlockSpec(memory_space=pltpu.SMEM)
    dma = pltpu.SemaphoreType.DMA
    image = pl.pallas_call(
        functools.partial(kernel, nblock, nshot),
        out_shape=jax.ShapeDtypeStruct((bx, bys, bz // nshot), f32),
        in_specs=[hbm, hbm, hbm, smem, smem, smem, hbm, hbm],
        out_specs=vmem,
        scratch_shapes=[
            pltpu.VMEM((STEPS, width + 8, 24, bz), f32),
            pltpu.VMEM((STEPS, width + 8, 24, bz), f32),
            pltpu.VMEM((width, bys, bz), f32),
            pltpu.VMEM((width, bys, bz), f32),
            pltpu.VMEM((width, bys, bz), f32),
            pltpu.VMEM((width, bys, bz), f32),
            pltpu.VMEM((bx, bys, bz), f32),
            pltpu.VMEM((STEPS, bys, bz), f32),
            pltpu.VMEM((2 * bz, 2 * bz), bf16),
            pltpu.VMEM((NB, bx, bys, bz), f32),
            pltpu.VMEM((2 * nshot, bx // nshot, bys, bz), f32),
            pltpu.VMEM((bx, bys, bz), f32),
            pltpu.VMEM((2 * width * bys, bz), bf16),
            pltpu.VMEM((2 * width * bys, bz), bf16),
            pltpu.VMEM((STEPS, bys, width), f32),
            pltpu.VMEM((bys, width), jnp.int32),
            pltpu.VMEM((bx * bys, bz), jnp.int16),
            pltpu.VMEM((NB, bx * bys, bz), jnp.int16),
            dma((5,)),
            dma((NB,)), dma((NB,)),
            dma((STEPS, NB)), dma((STEPS, NB)),
            dma((STEPS, NB)), dma((STEPS, NB)),
            dma((NB,)), dma((NB,)),
            dma((nshot,)), dma((nshot,)),
        ],
        compiler_params=pltpu.CompilerParams(
            collective_id=0, has_side_effects=True, vmem_limit_bytes=63 * 1024 * 1024),
    )(vel_sq[0], fwd_state.reshape(-1, bz), adj_state.reshape(-1, bz), wavelet, source, aperture,
      rec_mask[0].T, rec_data[0].transpose(0, 2, 1))
    return image[None]


def solution(mesh):
    placed = (
        P(("parts", "block"), None, "sub", None),
        P(("parts", "block", "shot"), None, None, "sub", None),
        P(("parts", "block", "shot"), None, None, "sub", None),
        P(("parts", "block", "shot"), None),
        P(("parts", "block", "shot"), None),
        P(("parts", "block", "shot"), None),
        P(("parts", "block", "shot"), None, "sub"),
        P(("parts", "block", "shot"), None, None, "sub"),
    )
    return jax.shard_map(
        functools.partial(shards, mesh.shape["block"], mesh.shape["shot"]),
        mesh=mesh,
        in_specs=placed,
        out_specs=P(("parts", "block"), None, "sub", "shot"),
        check_vma=False,
    )
```

```python
import functools

import jax
import jax.numpy as jnp
from jax import lax
from jax.experimental import pallas as pl
from jax.experimental.pallas import tpu as pltpu
from jax.sharding import PartitionSpec as P

R = 2
STEPS = 4
NB = 2 * R + 1
MESH = pl.DeviceIdType.MESH

coeffs = (-205.0 / 72.0, 8.0 / 5.0, -1.0 / 5.0, 8.0 / 315.0, -1.0 / 560.0)
image_scale = 0.05
vel_mid = 0.12
vel_step = 0.06 / 32000.0
f32 = jnp.float32
bf16 = jnp.bfloat16


def kernel(nblock, nshot, vel, fwd, adj, wav, src, ap, mask, rec, out,
           F, A, W, ZF, ZA, PV, O, T, B, G, SP, SR, M, FI, AI, RI, MI, VC, VG,
           ls, vs, vr, fs, fr, as_, ar, gs, gr, ss, sr):
    bx, bys, bz = vel.shape
    home = lax.axis_index("block")
    team = lax.axis_index("shot")
    sub = lax.axis_index("sub")
    lo = jnp.maximum(R - home, 0)
    hi = jnp.minimum(R + nblock - home, NB)
    n = hi - lo
    offsets = [o for o in range(-R, R + 1) if o != 0]
    down = (2 * home < nblock).astype(jnp.int32)
    first = down * (hi - 1) + (1 - down) * lo
    turn = 1 - 2 * down

    def near(o):
        return (home + o >= 0) & (home + o < nblock)

    barrier = pltpu.get_barrier_semaphore()
    for o in offsets:
        @pl.when(near(o))
        def _():
            pl.semaphore_signal(barrier, inc=1, device_id={"block": home + o}, device_id_type=MESH)
    for r in range(1, nshot):
        pl.semaphore_signal(barrier, inc=1, device_id={"shot": lax.rem(team + r, nshot)}, device_id_type=MESH)
    pl.semaphore_signal(barrier, inc=1, device_id={"sub": 1 - sub}, device_id_type=MESH)

    local = [pltpu.make_async_copy(fwd, FI, ls.at[0]), pltpu.make_async_copy(adj, AI, ls.at[1]),
             pltpu.make_async_copy(rec, RI, ls.at[2]), pltpu.make_async_copy(mask, MI, ls.at[3]),
             pltpu.make_async_copy(vel, W.at[pl.ds(R * bx, bx)], ls.at[4])]
    for copy in local[::-1]:
        copy.start()

    def keep_of(b):
        return jnp.where((b >= R - ap[0, 0]) & (b <= R + ap[0, 1]), 1.0, 0.0).astype(f32)

    def at(field, t, b):
        return field[t, pl.ds(4 + b * bx, bx), 8:16, :]

    def state(ref, t, b):
        rows = pl.ds(pl.multiple_of(t * NB * bx * bys + b * bx * bys, bx * bys), bx * bys)
        return ref[rows, :].astype(f32).reshape(bx, bys, bz)

    zx = jnp.zeros((4, 8, bz), f32)

    @pl.when(sub == 0)
    def _():
        lax.fori_loop(lo, hi, functools.partial(clear_at, F, A, 0, bx, bz), 0)

    @pl.when(sub == 1)
    def _():
        lax.fori_loop(lo, hi, functools.partial(clear_at, F, A, 16, bx, bz), 0)

    for field in (F, A):
        for t in range(STEPS):
            field[t, pl.ds(lo * bx, 4), 8:16, :] = zx
            field[t, pl.ds(4 + hi * bx, 4), 8:16, :] = zx

    local[4].wait()
    code = jnp.round((W[R * bx:(R + 1) * bx].reshape(bx * bys, bz) - vel_mid) * (1.0 / vel_step))
    VC[...] = code.astype(jnp.int32).astype(jnp.int16)

    pl.semaphore_wait(barrier, (n - 1) + (nshot - 1) + 1)

    def vel_copy(o):
        j = R - o
        return pltpu.make_async_remote_copy(
            src_ref=VC, dst_ref=VG.at[j], send_sem=vs.at[j], recv_sem=vr.at[j],
            device_id={"block": home + o}, device_id_type=MESH)

    for o in (-2, 2, -1, 1):
        @pl.when(near(o))
        def _():
            vel_copy(o).start()

    def rim(side, field, t, b, ssem, rsem):
        x = pl.ds(4 + b * bx, bx)
        return pltpu.make_async_remote_copy(
            src_ref=field.at[t, x, pl.ds(8 if side else 12, 4), :],
            dst_ref=field.at[t, x, pl.ds(16 if side else 4, 4), :],
            send_sem=ssem.at[t, b], recv_sem=rsem.at[t, b],
            device_id={"sub": 1 - sub}, device_id_type=MESH)

    def rim_start(t, b):
        for side in range(2):
            @pl.when(sub == side)
            def _():
                rim(side, F, t, b, fs, fr).start()
                rim(side, A, t, b, as_, ar).start()

    def rim_wait(t, b):
        for side in range(2):
            @pl.when(sub == side)
            def _():
                rim(1 - side, F, t, b, fs, fr).wait_recv()
                rim(1 - side, A, t, b, as_, ar).wait_recv()

    def rim_sent(t, b):
        for side in range(2):
            @pl.when(sub == side)
            def _():
                rim(side, F, t, b, fs, fr).wait_send()
                rim(side, A, t, b, as_, ar).wait_send()

    local[0].wait()
    local[1].wait()

    def load_states(i, c):
        b = first + turn * i
        kb = keep_of(b)
        rows = pl.ds(4 + b * bx, bx)
        F[0, rows, 8:16, :] = kb * state(FI, 1, b)
        A[0, rows, 8:16, :] = kb * state(AI, 1, b)
        rim_start(0, b)
        return c

    lax.fori_loop(0, n, load_states, 0)

    i0 = lax.broadcasted_iota(jnp.int32, (bz, bz), 0)
    i1 = lax.broadcasted_iota(jnp.int32, (bz, bz), 1)
    dist = jnp.abs(i0 - i1)
    band = jnp.where(dist == 0, 3.0 * coeffs[0], 0.0).astype(f32)
    for j in range(1, 5):
        band = jnp.where(dist == j, coeffs[j], band)
    band_hi = band.astype(bf16)
    band_lo = (band - band_hi.astype(f32)).astype(bf16)
    B[0:bz, 0:bz] = band_hi
    B[bz:2 * bz, 0:bz] = band_hi
    B[0:bz, bz:2 * bz] = band_lo
    B[bz:2 * bz, bz:2 * bz] = jnp.zeros((bz, bz), bf16)

    ox = lax.broadcasted_iota(jnp.int32, (bx, bys, bz), 0)
    oy = lax.broadcasted_iota(jnp.int32, (bx, bys, bz), 1) + sub * bys
    oz = lax.broadcasted_iota(jnp.int32, (bx, bys, bz), 2)
    O[...] = jnp.where((ox == src[0, 0]) & (oy == src[0, 1]) & (oz == src[0, 2]), 1.0, 0.0).astype(f32)
    local[2].wait()
    local[3].wait()
    live = MI[...].astype(f32)
    T[...] = jnp.zeros_like(T)
    for t in range(STEPS):
        T[t, :, 0:NB * bx] = live * RI[t]
    surface = lax.broadcasted_iota(jnp.int32, (bys, bz), 1) == 0

    def laplace(t, b):
        flat = jnp.concatenate([at(F, t, b).reshape(bx * bys, bz), at(A, t, b).reshape(bx * bys, bz)], axis=0)
        high = flat.astype(bf16)
        low = (flat - high.astype(f32)).astype(bf16)
        both = jnp.concatenate([high, low], axis=1)
        prod = jnp.dot(both, B[...], preferred_element_type=f32)
        depth = prod[:, :bz] + prod[:, bz:]
        result = []
        for k, field in enumerate((F, A)):
            total = depth[k * bx * bys:(k + 1) * bx * bys].reshape(bx, bys, bz)
            for j in range(1, 5):
                total = total + coeffs[j] * (
                    field[t, pl.ds(4 + j + b * bx, bx), 8:16, :] + field[t, pl.ds(4 - j + b * bx, bx), 8:16, :]
                    + field[t, pl.ds(4 + b * bx, bx), 8 + j:16 + j, :] + field[t, pl.ds(4 + b * bx, bx), 8 - j:16 - j, :])
            result.append(total)
        return result

    def source_term(step, b):
        return jnp.where(b == R, wav[0, step], 0.0) * O[...]

    def receiver_term(step, b):
        row = pltpu.roll(T[STEPS - 1 - step], 128 - b * bx, 1) * keep_of(b)
        parts = []
        for x in range(bx):
            moved = pltpu.roll(row, 128 - x, 1) if x else row
            parts.append(jnp.where(surface, moved, 0.0)[None])
        return jnp.concatenate(parts, axis=0)

    def first_diff(i, c):
        b = first + turn * i
        rim_wait(0, b)
        cells = pl.ds(b * bx, bx)
        ZF[cells], ZA[cells] = laplace(0, b)
        return c

    lax.fori_loop(0, n, first_diff, 0)

    def image_copy(j):
        return pltpu.make_async_remote_copy(
            src_ref=M.at[j], dst_ref=G.at[j], send_sem=gs.at[j], recv_sem=gr.at[j],
            device_id={"block": home + j - R}, device_id_type=MESH)

    zl = bz // nshot
    xg = bx // nshot
    lane = lax.broadcasted_iota(jnp.int32, (xg, bys, bz), 2)

    def packed(b, d):
        total = jnp.zeros((xg, bys, bz), f32)
        for k in range(nshot):
            shift = lax.rem((k - d + nshot) * zl, bz)
            layers = PV[pl.ds(b * bx + k * xg, xg)].reshape(xg * bys, bz)
            moved = pltpu.roll(layers, shift, 1).reshape(xg, bys, bz)
            total = jnp.where((lane >= k * zl) & (lane < (k + 1) * zl), moved, total)
        return total

    def team_copy(b, r):
        return pltpu.make_async_remote_copy(
            src_ref=SP.at[b, r], dst_ref=SR.at[b, r], send_sem=ss.at[b, r], recv_sem=sr.at[b, r],
            device_id={"shot": lax.rem(team + r, nshot)}, device_id_type=MESH)

    def finish(b):
        total = M[b]
        for r in range(1, nshot):
            team_copy(b, r).wait_recv()
            total = total + SR[b, r]
        M[b] = total

        @pl.when(b != R)
        def _():
            image_copy(b).start()

    def vel_wait(b):
        pltpu.make_async_remote_copy(
            src_ref=VC, dst_ref=VG.at[b], send_sem=vs.at[b], recv_sem=vr.at[b],
            device_id={"block": home + b - R}, device_id_type=MESH).wait_recv()

    def advance(step, b):
        last = step == STEPS - 1
        cells = pl.ds(b * bx, bx)
        if step == 0:
            @pl.when(b != R)
            def _():
                vel_wait(b)
                W[cells] = (VG[b].astype(jnp.int32).astype(f32) * vel_step + vel_mid).reshape(bx, bys, bz)
            kb = keep_of(b)
            w = kb * W[cells]
            W[cells] = w
            lap_f, lap_a = ZF[cells], ZA[cells]
            old_f, old_a = kb * state(FI, 0, b), kb * state(AI, 0, b)
        else:
            rim_wait(step, b)
            w = W[cells]
            lap_f, lap_a = laplace(step, b)
            old_f, old_a = at(F, step - 1, b), at(A, step - 1, b)
        new_f = 2.0 * at(F, step, b) - old_f + w * lap_f + source_term(step, b)
        new_a = 2.0 * at(A, step, b) - old_a + w * lap_a + receiver_term(step, b)
        if not last:
            F[step + 1, pl.ds(4 + b * bx, bx), 8:16, :] = new_f
            A[step + 1, pl.ds(4 + b * bx, bx), 8:16, :] = new_a
            rim_start(step + 1, b)
        if step == 1:
            PV[cells] = new_f * new_a
        elif step > 1:
            early = STEPS - 1 - step
            PV[cells] = PV[cells] + new_f * at(A, early, b) + at(F, early, b) * new_a
        if last:
            for r in range(1, nshot):
                SP[b, r] = packed(b, lax.rem(team + r, nshot))
                team_copy(b, r).start()
            M[b] = packed(b, team)

    def wave(k, c):
        for step in range(STEPS):
            @pl.when((k >= step) & (k - step < n))
            def _():
                advance(step, first + turn * (k - step))

        @pl.when(k >= STEPS)
        def _():
            finish(first + turn * (k - STEPS))
        return c

    lax.fori_loop(0, n + STEPS, wave, 0)

    for o in (-1, 1, -2, 2):
        @pl.when(near(o))
        def _():
            j = R - o
            image_copy(j).wait_recv()
            M[R] = M[R] + G[j]

    total = M[R]
    total = image_scale * total
    for k in range(nshot):
        flat = total.reshape(xg * bys, bz)
        moved = pltpu.roll(flat, bz - k * zl, 1) if k else flat
        out[k * xg:(k + 1) * xg] = moved.reshape(xg, bys, bz)[:, :, :zl]

    def sent(b, c):
        for t in range(STEPS):
            rim_sent(t, b)
        for r in range(1, nshot):
            team_copy(b, r).wait_send()
        return c

    lax.fori_loop(lo, hi, sent, 0)
    for o in offsets:
        @pl.when(near(o))
        def _():
            vel_copy(o).wait_send()
            image_copy(R + o).wait_send()


def clear_at(F, A, row, bx, bz, b, c):
    for field in (F, A):
        for t in range(STEPS):
            field[t, pl.ds(4 + b * bx, bx), row:row + 8, :] = jnp.zeros((bx, 8, bz), f32)
    return c


def shards(nblock, nshot, vel_sq, fwd_state, adj_state, wavelet, source, aperture, rec_mask, rec_data):
    bx, bys, bz = vel_sq.shape[1:]
    width = NB * bx
    vmem = pl.BlockSpec(memory_space=pltpu.VMEM)
    hbm = pl.BlockSpec(memory_space=pltpu.HBM)
    smem = pl.BlockSpec(memory_space=pltpu.SMEM)
    dma = pltpu.SemaphoreType.DMA
    image = pl.pallas_call(
        functools.partial(kernel, nblock, nshot),
        out_shape=jax.ShapeDtypeStruct((bx, bys, bz // nshot), f32),
        in_specs=[hbm, hbm, hbm, smem, smem, smem, hbm, hbm],
        out_specs=vmem,
        scratch_shapes=[
            pltpu.VMEM((STEPS, width + 8, 24, bz), f32),
            pltpu.VMEM((STEPS, width + 8, 24, bz), f32),
            pltpu.VMEM((width, bys, bz), f32),
            pltpu.VMEM((width, bys, bz), f32),
            pltpu.VMEM((width, bys, bz), f32),
            pltpu.VMEM((width, bys, bz), f32),
            pltpu.VMEM((bx, bys, bz), f32),
            pltpu.VMEM((STEPS, bys, bz), f32),
            pltpu.VMEM((2 * bz, 2 * bz), bf16),
            pltpu.VMEM((NB, bx // nshot, bys, bz), f32),
            pltpu.VMEM((NB, nshot, bx // nshot, bys, bz), f32),
            pltpu.VMEM((NB, nshot, bx // nshot, bys, bz), f32),
            pltpu.VMEM((NB, bx // nshot, bys, bz), f32),
            pltpu.VMEM((2 * width * bys, bz), bf16),
            pltpu.VMEM((2 * width * bys, bz), bf16),
            pltpu.VMEM((STEPS, bys, width), f32),
            pltpu.VMEM((bys, width), jnp.int32),
            pltpu.VMEM((bx * bys, bz), jnp.int16),
            pltpu.VMEM((NB, bx * bys, bz), jnp.int16),
            dma((5,)),
            dma((NB,)), dma((NB,)),
            dma((STEPS, NB)), dma((STEPS, NB)),
            dma((STEPS, NB)), dma((STEPS, NB)),
            dma((NB,)), dma((NB,)),
            dma((NB, nshot)), dma((NB, nshot)),
        ],
        compiler_params=pltpu.CompilerParams(
            collective_id=0, has_side_effects=True, vmem_limit_bytes=63 * 1024 * 1024),
    )(vel_sq[0], fwd_state.reshape(-1, bz), adj_state.reshape(-1, bz), wavelet, source, aperture,
      rec_mask[0].T, rec_data[0].transpose(0, 2, 1))
    return image[None]


def solution(mesh):
    placed = (
        P(("parts", "block"), None, "sub", None),
        P(("parts", "block", "shot"), None, None, "sub", None),
        P(("parts", "block", "shot"), None, None, "sub", None),
        P(("parts", "block", "shot"), None),
        P(("parts", "block", "shot"), None),
        P(("parts", "block", "shot"), None),
        P(("parts", "block", "shot"), None, "sub"),
        P(("parts", "block", "shot"), None, None, "sub"),
    )
    return jax.shard_map(
        functools.partial(shards, mesh.shape["block"], mesh.shape["shot"]),
        mesh=mesh,
        in_specs=placed,
        out_specs=P(("parts", "block"), None, "sub", "shot"),
        check_vma=False,
    )
```

```python
import functools

import jax
import jax.numpy as jnp
from jax import lax
from jax.experimental import pallas as pl
from jax.experimental.pallas import tpu as pltpu
from jax.sharding import PartitionSpec as P

R = 2
STEPS = 4
NB = 2 * R + 1
MESH = pl.DeviceIdType.MESH

coeffs = (-205.0 / 72.0, 8.0 / 5.0, -1.0 / 5.0, 8.0 / 315.0, -1.0 / 560.0)
image_scale = 0.05
vel_mid = 0.12
vel_step = 0.06 / 32000.0
f32 = jnp.float32
bf16 = jnp.bfloat16


def kernel(nblock, nshot, vel, fwd, adj, wav, src, ap, mask, rec, out,
           FA, W, ZF, ZA, PV, O, T, B, G, S, H, FI, AI, RI, MI, VC, VG,
           ls, vs, vr, fs, fr, gs, gr, ss, sr):
    bx, bys, bz = vel.shape
    F, A = FA.at[:, 0], FA.at[:, 1]
    home = lax.axis_index("block")
    team = lax.axis_index("shot")
    sub = lax.axis_index("sub")
    lo = jnp.maximum(R - home, 0)
    hi = jnp.minimum(R + nblock - home, NB)
    n = hi - lo
    offsets = [o for o in range(-R, R + 1) if o != 0]
    down = (2 * home < nblock).astype(jnp.int32)
    first = down * (hi - 1) + (1 - down) * lo
    turn = 1 - 2 * down

    def near(o):
        return (home + o >= 0) & (home + o < nblock)

    barrier = pltpu.get_barrier_semaphore()
    for o in offsets:
        @pl.when(near(o))
        def _():
            pl.semaphore_signal(barrier, inc=1, device_id={"block": home + o}, device_id_type=MESH)
    for r in range(1, nshot):
        pl.semaphore_signal(barrier, inc=1, device_id={"shot": lax.rem(team + r, nshot)}, device_id_type=MESH)
    pl.semaphore_signal(barrier, inc=1, device_id={"sub": 1 - sub}, device_id_type=MESH)

    local = [pltpu.make_async_copy(fwd, FI, ls.at[0]), pltpu.make_async_copy(adj, AI, ls.at[1]),
             pltpu.make_async_copy(rec, RI, ls.at[2]), pltpu.make_async_copy(mask, MI, ls.at[3]),
             pltpu.make_async_copy(vel, W.at[pl.ds(R * bx, bx)], ls.at[4])]
    for copy in local[::-1]:
        copy.start()

    def keep_of(b):
        return jnp.where((b >= R - ap[0, 0]) & (b <= R + ap[0, 1]), 1.0, 0.0).astype(f32)

    def at(field, t, b):
        return field[t, pl.ds(4 + b * bx, bx), 8:16, :]

    def state(ref, t, b):
        rows = pl.ds(pl.multiple_of(t * NB * bx * bys + b * bx * bys, bx * bys), bx * bys)
        return ref[rows, :].astype(f32).reshape(bx, bys, bz)

    zx = jnp.zeros((4, 8, bz), f32)

    @pl.when(sub == 0)
    def _():
        lax.fori_loop(lo, hi, functools.partial(clear_at, F, A, 0, bx, bz), 0)

    @pl.when(sub == 1)
    def _():
        lax.fori_loop(lo, hi, functools.partial(clear_at, F, A, 16, bx, bz), 0)

    for field in (F, A):
        for t in range(STEPS):
            field[t, pl.ds(lo * bx, 4), 8:16, :] = zx
            field[t, pl.ds(4 + hi * bx, 4), 8:16, :] = zx

    local[4].wait()
    code = jnp.round((W[R * bx:(R + 1) * bx].reshape(bx * bys, bz) - vel_mid) * (1.0 / vel_step))
    VC[...] = code.astype(jnp.int32).astype(jnp.int16)

    pl.semaphore_wait(barrier, (n - 1) + (nshot - 1) + 1)

    def vel_copy(o):
        j = R - o
        return pltpu.make_async_remote_copy(
            src_ref=VC, dst_ref=VG.at[j], send_sem=vs.at[j], recv_sem=vr.at[j],
            device_id={"block": home + o}, device_id_type=MESH)

    for o in (-2, 2, -1, 1):
        @pl.when(near(o))
        def _():
            vel_copy(o).start()

    def rim(side, t, b):
        x = pl.ds(4 + b * bx, bx)
        return pltpu.make_async_remote_copy(
            src_ref=FA.at[t, :, x, pl.ds(8 if side else 12, 4), :],
            dst_ref=FA.at[t, :, x, pl.ds(16 if side else 4, 4), :],
            send_sem=fs.at[t, b], recv_sem=fr.at[t, b],
            device_id={"sub": 1 - sub}, device_id_type=MESH)

    def rim_start(t, b):
        for side in range(2):
            @pl.when(sub == side)
            def _():
                rim(side, t, b).start()

    def rim_wait(t, b):
        for side in range(2):
            @pl.when(sub == side)
            def _():
                rim(1 - side, t, b).wait_recv()

    def rim_sent(t, b):
        for side in range(2):
            @pl.when(sub == side)
            def _():
                rim(side, t, b).wait_send()

    local[0].wait()
    local[1].wait()

    def load_states(i, c):
        b = first + turn * i
        kb = keep_of(b)
        rows = pl.ds(4 + b * bx, bx)
        F[0, rows, 8:16, :] = kb * state(FI, 1, b)
        A[0, rows, 8:16, :] = kb * state(AI, 1, b)
        rim_start(0, b)
        return c

    lax.fori_loop(0, n, load_states, 0)

    i0 = lax.broadcasted_iota(jnp.int32, (bz, bz), 0)
    i1 = lax.broadcasted_iota(jnp.int32, (bz, bz), 1)
    dist = jnp.abs(i0 - i1)
    band = jnp.where(dist == 0, 3.0 * coeffs[0], 0.0).astype(f32)
    for j in range(1, 5):
        band = jnp.where(dist == j, coeffs[j], band)
    band_hi = band.astype(bf16)
    band_lo = (band - band_hi.astype(f32)).astype(bf16)
    B[0:bz, 0:bz] = band_hi
    B[bz:2 * bz, 0:bz] = band_hi
    B[0:bz, bz:2 * bz] = band_lo
    B[bz:2 * bz, bz:2 * bz] = jnp.zeros((bz, bz), bf16)

    ox = lax.broadcasted_iota(jnp.int32, (bx, bys, bz), 0)
    oy = lax.broadcasted_iota(jnp.int32, (bx, bys, bz), 1) + sub * bys
    oz = lax.broadcasted_iota(jnp.int32, (bx, bys, bz), 2)
    O[...] = jnp.where((ox == src[0, 0]) & (oy == src[0, 1]) & (oz == src[0, 2]), 1.0, 0.0).astype(f32)
    local[2].wait()
    local[3].wait()
    live = MI[...].astype(f32)
    T[...] = jnp.zeros_like(T)
    for t in range(STEPS):
        T[t, :, 0:NB * bx] = live * RI[t]
    surface = lax.broadcasted_iota(jnp.int32, (bys, bz), 1) == 0

    def laplace(t, b):
        flat = jnp.concatenate([at(F, t, b).reshape(bx * bys, bz), at(A, t, b).reshape(bx * bys, bz)], axis=0)
        high = flat.astype(bf16)
        low = (flat - high.astype(f32)).astype(bf16)
        both = jnp.concatenate([high, low], axis=1)
        prod = jnp.dot(both, B[...], preferred_element_type=f32)
        depth = prod[:, :bz] + prod[:, bz:]
        result = []
        for k, field in enumerate((F, A)):
            total = depth[k * bx * bys:(k + 1) * bx * bys].reshape(bx, bys, bz)
            for j in range(1, 5):
                total = total + coeffs[j] * (
                    field[t, pl.ds(4 + j + b * bx, bx), 8:16, :] + field[t, pl.ds(4 - j + b * bx, bx), 8:16, :]
                    + field[t, pl.ds(4 + b * bx, bx), 8 + j:16 + j, :] + field[t, pl.ds(4 + b * bx, bx), 8 - j:16 - j, :])
            result.append(total)
        return result

    def source_term(step, b):
        return jnp.where(b == R, wav[0, step], 0.0) * O[...]

    def receiver_term(step, b):
        row = pltpu.roll(T[STEPS - 1 - step], 128 - b * bx, 1) * keep_of(b)
        parts = []
        for x in range(bx):
            moved = pltpu.roll(row, 128 - x, 1) if x else row
            parts.append(jnp.where(surface, moved, 0.0)[None])
        return jnp.concatenate(parts, axis=0)

    def first_diff(i, c):
        b = first + turn * i
        rim_wait(0, b)
        cells = pl.ds(b * bx, bx)
        ZF[cells], ZA[cells] = laplace(0, b)
        return c

    lax.fori_loop(0, n, first_diff, 0)

    def image_copy(j):
        return pltpu.make_async_remote_copy(
            src_ref=PV.at[pl.ds(j * bx, bx)], dst_ref=G.at[j], send_sem=gs.at[j], recv_sem=gr.at[j],
            device_id={"block": home + j - R}, device_id_type=MESH)

    def vel_wait(b):
        pltpu.make_async_remote_copy(
            src_ref=VC, dst_ref=VG.at[b], send_sem=vs.at[b], recv_sem=vr.at[b],
            device_id={"block": home + b - R}, device_id_type=MESH).wait_recv()

    def advance(step, b):
        last = step == STEPS - 1
        cells = pl.ds(b * bx, bx)
        if step == 0:
            @pl.when(b != R)
            def _():
                vel_wait(b)
                W[cells] = (VG[b].astype(jnp.int32).astype(f32) * vel_step + vel_mid).reshape(bx, bys, bz)
            kb = keep_of(b)
            w = kb * W[cells]
            W[cells] = w
            lap_f, lap_a = ZF[cells], ZA[cells]
            old_f, old_a = kb * state(FI, 0, b), kb * state(AI, 0, b)
        else:
            rim_wait(step, b)
            w = W[cells]
            lap_f, lap_a = laplace(step, b)
            old_f, old_a = at(F, step - 1, b), at(A, step - 1, b)
        new_f = 2.0 * at(F, step, b) - old_f + w * lap_f + source_term(step, b)
        new_a = 2.0 * at(A, step, b) - old_a + w * lap_a + receiver_term(step, b)
        if not last:
            F[step + 1, pl.ds(4 + b * bx, bx), 8:16, :] = new_f
            A[step + 1, pl.ds(4 + b * bx, bx), 8:16, :] = new_a
            rim_start(step + 1, b)
        if step == 1:
            PV[cells] = new_f * new_a
        elif step > 1:
            early = STEPS - 1 - step
            PV[cells] = PV[cells] + new_f * at(A, early, b) + at(F, early, b) * new_a
        if last:
            @pl.when(b != R)
            def _():
                image_copy(b).start()

    def wave(k, c):
        for step in range(STEPS):
            @pl.when((k >= step) & (k - step < n))
            def _():
                advance(step, first + turn * (k - step))
        return c

    lax.fori_loop(0, n + STEPS - 1, wave, 0)

    H[...] = PV[R * bx:(R + 1) * bx]
    for o in (-1, 1, -2, 2):
        @pl.when(near(o))
        def _():
            j = R - o
            image_copy(j).wait_recv()
            H[...] = H[...] + G[j]

    zl = bz // nshot
    xg = bx // nshot
    lane = lax.broadcasted_iota(jnp.int32, (xg, bys, bz), 2)

    def packed(d):
        total = jnp.zeros((xg, bys, bz), f32)
        for k in range(nshot):
            shift = lax.rem((k - d + nshot) * zl, bz)
            moved = pltpu.roll(H[k * xg:(k + 1) * xg].reshape(xg * bys, bz), shift, 1).reshape(xg, bys, bz)
            total = jnp.where((lane >= k * zl) & (lane < (k + 1) * zl), moved, total)
        return total

    def team_copy(r):
        return pltpu.make_async_remote_copy(
            src_ref=S.at[r], dst_ref=S.at[nshot + r], send_sem=ss.at[r], recv_sem=sr.at[r],
            device_id={"shot": lax.rem(team + r, nshot)}, device_id_type=MESH)

    for r in range(1, nshot):
        S[r] = packed(lax.rem(team + r, nshot))
        team_copy(r).start()
    total = packed(team)
    for r in range(1, nshot):
        team_copy(r).wait_recv()
        total = total + S[nshot + r]
    total = image_scale * total
    for k in range(nshot):
        flat = total.reshape(xg * bys, bz)
        moved = pltpu.roll(flat, bz - k * zl, 1) if k else flat
        out[k * xg:(k + 1) * xg] = moved.reshape(xg, bys, bz)[:, :, :zl]

    def sent(b, c):
        for t in range(STEPS):
            rim_sent(t, b)
        return c

    lax.fori_loop(lo, hi, sent, 0)
    for o in offsets:
        @pl.when(near(o))
        def _():
            vel_copy(o).wait_send()
            image_copy(R + o).wait_send()
    for r in range(1, nshot):
        team_copy(r).wait_send()


def clear_at(F, A, row, bx, bz, b, c):
    for field in (F, A):
        for t in range(STEPS):
            field[t, pl.ds(4 + b * bx, bx), row:row + 8, :] = jnp.zeros((bx, 8, bz), f32)
    return c


def shards(nblock, nshot, vel_sq, fwd_state, adj_state, wavelet, source, aperture, rec_mask, rec_data):
    bx, bys, bz = vel_sq.shape[1:]
    width = NB * bx
    vmem = pl.BlockSpec(memory_space=pltpu.VMEM)
    hbm = pl.BlockSpec(memory_space=pltpu.HBM)
    smem = pl.BlockSpec(memory_space=pltpu.SMEM)
    dma = pltpu.SemaphoreType.DMA
    image = pl.pallas_call(
        functools.partial(kernel, nblock, nshot),
        out_shape=jax.ShapeDtypeStruct((bx, bys, bz // nshot), f32),
        in_specs=[hbm, hbm, hbm, smem, smem, smem, hbm, hbm],
        out_specs=vmem,
        scratch_shapes=[
            pltpu.VMEM((STEPS, 2, width + 8, 24, bz), f32),
            pltpu.VMEM((width, bys, bz), f32),
            pltpu.VMEM((width, bys, bz), f32),
            pltpu.VMEM((width, bys, bz), f32),
            pltpu.VMEM((width, bys, bz), f32),
            pltpu.VMEM((bx, bys, bz), f32),
            pltpu.VMEM((STEPS, bys, bz), f32),
            pltpu.VMEM((2 * bz, 2 * bz), bf16),
            pltpu.VMEM((NB, bx, bys, bz), f32),
            pltpu.VMEM((2 * nshot, bx // nshot, bys, bz), f32),
            pltpu.VMEM((bx, bys, bz), f32),
            pltpu.VMEM((2 * width * bys, bz), bf16),
            pltpu.VMEM((2 * width * bys, bz), bf16),
            pltpu.VMEM((STEPS, bys, width), f32),
            pltpu.VMEM((bys, width), jnp.int32),
            pltpu.VMEM((bx * bys, bz), jnp.int16),
            pltpu.VMEM((NB, bx * bys, bz), jnp.int16),
            dma((5,)),
            dma((NB,)), dma((NB,)),
            dma((STEPS, NB)), dma((STEPS, NB)),
            dma((NB,)), dma((NB,)),
            dma((nshot,)), dma((nshot,)),
        ],
        compiler_params=pltpu.CompilerParams(
            collective_id=0, has_side_effects=True, vmem_limit_bytes=63 * 1024 * 1024),
    )(vel_sq[0], fwd_state.reshape(-1, bz), adj_state.reshape(-1, bz), wavelet, source, aperture,
      rec_mask[0].T, rec_data[0].transpose(0, 2, 1))
    return image[None]


def solution(mesh):
    placed = (
        P(("parts", "block"), None, "sub", None),
        P(("parts", "block", "shot"), None, None, "sub", None),
        P(("parts", "block", "shot"), None, None, "sub", None),
        P(("parts", "block", "shot"), None),
        P(("parts", "block", "shot"), None),
        P(("parts", "block", "shot"), None),
        P(("parts", "block", "shot"), None, "sub"),
        P(("parts", "block", "shot"), None, None, "sub"),
    )
    return jax.shard_map(
        functools.partial(shards, mesh.shape["block"], mesh.shape["shot"]),
        mesh=mesh,
        in_specs=placed,
        out_specs=P(("parts", "block"), None, "sub", "shot"),
        check_vma=False,
    )
```
